32 devices in a mesh: seq: 16 (over z, x, core), head: 2 (over y).
Axes of the slice: x: 2, y: 2, z: 4, core: 2. Of those that a mesh axis runs over, the one named last changes fastest.
Arguments:
- queries: bfloat16 [16384, 5120], P(('seq', 'head')), may hold values from -7.5 to 7.5
- keys: bfloat16 [16384, 1024], P(('seq', 'head')), may hold values from -7.5 to 7.5
- values: bfloat16 [16384, 1024], P(('seq', 'head')), may hold values from -6 to 6
- fetch_list: int32 [16, 16, 2], replicated, may hold values from 0 to 15, as said below
- choose: int32 [256, 16], P('seq'), may hold values from 0 to 31, as said below
- live: int32 [256], P('seq'), may hold values from 0 to 16, as said below
Outputs:
- attn_out: bfloat16 [16384, 5120], P(('seq', 'head'))
The draws below stay inside these ranges and needn't reach their ends.
Inputs may be any that keep to these rules, and one draw needn't show every extreme that they name: Each row fetch_list[d, s] holds 2 distinct blocks. Each row of choose holds 16 distinct slots; slot j stands for entry j % 2 of fetch_list[d, j // 2]; the first live[b] entries of row b name slots j with j // 2 < b // 16. live[b] is at most 2 * (b // 16); every draw has a block with live equal to 16.
All inputs are finite; a program needn't handle non-finite values.
Results may differ from the reference program's by a relative error of at most 0.0042.
Values may be sent and summed in bfloat16 or wider, within the bound.
No kernel may reach another device: no remote copies, remote signals or barrier semaphores. Data moves between devices by JAX's collectives and lax.ppermute only.
A program may use at most 64 MiB of HBM per device.

```python
import math
import jax
import jax.numpy as jnp
from jax import lax

QUERY_HEADS = 40
KEY_VALUE_HEADS = 8
HEAD_WIDTH = 128
BLOCK_TOKENS = 64
CAP = 2
LISTED_ENTRIES = 16
TOK_DEV = 1024
CONTEXT_TOKENS = 16384
FILE_BLOCKS = 256
SLOTS = 32
N_SEQ = 16


def draw_keys(key, part):
    filled_slots = jax.random.normal(jax.random.fold_in(key, 11), (CONTEXT_TOKENS, KEY_VALUE_HEADS * HEAD_WIDTH), jnp.float32)
    return jnp.clip(filled_slots, -7.5, 7.5).astype(jnp.bfloat16)


def draw_queries(key, part):
    filled_slots = jax.random.normal(jax.random.fold_in(key, 12), (CONTEXT_TOKENS, QUERY_HEADS * HEAD_WIDTH), jnp.float32)
    return jnp.clip(filled_slots, -7.5, 7.5).astype(jnp.bfloat16)


def draw_fetch_list(key, part):
    blocks_per_dev = TOK_DEV // BLOCK_TOKENS
    ranking = jax.random.randint(jax.random.fold_in(key, 21), (N_SEQ, N_SEQ, blocks_per_dev), 0, 1 << 20)
    ranking = ranking * blocks_per_dev + jnp.arange(blocks_per_dev, dtype=jnp.int32)
    return lax.top_k(ranking, CAP)[1].astype(jnp.int32)


def draw_choose(key, part):
    blocks_per_dev = TOK_DEV // BLOCK_TOKENS
    ranking = jax.random.randint(jax.random.fold_in(key, 22), (FILE_BLOCKS, SLOTS), 0, 1 << 16)
    ranking = ranking * SLOTS + jnp.arange(SLOTS, dtype=jnp.int32)
    shard_of = jnp.arange(FILE_BLOCKS, dtype=jnp.int32) // blocks_per_dev
    earlier = (jnp.arange(SLOTS, dtype=jnp.int32) // CAP)[None, :] < shard_of[:, None]
    ranking = ranking + earlier.astype(jnp.int32) * (1 << 24)
    return lax.top_k(ranking, LISTED_ENTRIES)[1].astype(jnp.int32)


def draw_live(key, part):
    blocks_per_dev = TOK_DEV // BLOCK_TOKENS
    heavy_share = jax.random.randint(jax.random.fold_in(key, 31), (N_SEQ,), 0, 6)
    heavy_roll = jax.random.randint(jax.random.fold_in(key, 32), (FILE_BLOCKS,), 0, 16)
    heavy = heavy_roll < jnp.repeat(heavy_share, FILE_BLOCKS // N_SEQ, total_repeat_length=FILE_BLOCKS)
    light_count = jax.random.randint(jax.random.fold_in(key, 33), (FILE_BLOCKS,), 1, 4)
    heavy_count = jax.random.randint(jax.random.fold_in(key, 34), (FILE_BLOCKS,), LISTED_ENTRIES // 2, LISTED_ENTRIES + 1)
    forced = (N_SEQ - 1) * blocks_per_dev + jax.random.randint(jax.random.fold_in(key, 35), (), 0, blocks_per_dev)
    counts = jnp.where(heavy, heavy_count, light_count)
    limit = CAP * (jnp.arange(FILE_BLOCKS, dtype=jnp.int32) // blocks_per_dev)
    counts = jnp.minimum(counts, limit)
    counts = jnp.where(jnp.arange(FILE_BLOCKS) == forced, LISTED_ENTRIES, counts)
    return counts.astype(jnp.int32)


def block_scale(key, extent, shards, smallest, largest):
    factor_of = 1.0
    for axis_at, shards_of in shards:
        heights = jax.random.uniform(jax.random.fold_in(jax.random.fold_in(key, 6), axis_at), (shards_of,), jnp.float32, smallest / len(shards), largest / len(shards))
        factor_of = factor_of * jnp.repeat(jnp.exp(heights), extent[axis_at] // shards_of).reshape((-1,) + (1,) * (len(extent) - 1 - axis_at))
    return factor_of


def gaussian(own_key, dims, scale, most, pieces=(), kind=jnp.bfloat16):
    entries = scale * jax.random.normal(own_key, dims, jnp.float32)
    if pieces:
        entries = entries * block_scale(own_key, dims, pieces, -0.22, 0.18)
    return jnp.clip(entries, -most, most).astype(kind)


def setup_inputs(seed: int = 0) -> dict:
    streams_of = jax.random.split(jax.random.key(seed), 7)
    return {
        "queries": draw_queries(jax.random.fold_in(streams_of[6], 71), 0),
        "keys": draw_keys(jax.random.fold_in(streams_of[6], 71), 0),
        "values": gaussian(streams_of[2], (CONTEXT_TOKENS, KEY_VALUE_HEADS * HEAD_WIDTH), 1.0, 6.0, ((0, 32),)),
        "fetch_list": draw_fetch_list(jax.random.fold_in(streams_of[6], 71), 0),
        "choose": draw_choose(jax.random.fold_in(streams_of[6], 71), 0),
        "live": draw_live(jax.random.fold_in(streams_of[6], 71), 0),
    }


def reference(queries, keys, values, fetch_list, choose, live):
    blocks_per_dev = TOK_DEV // BLOCK_TOKENS
    repeat_factor = QUERY_HEADS // KEY_VALUE_HEADS
    scaling = 1.0 / math.sqrt(HEAD_WIDTH)
    query_block_rows = queries.reshape(FILE_BLOCKS, BLOCK_TOKENS, KEY_VALUE_HEADS, repeat_factor, HEAD_WIDTH)
    key_block_rows = keys.reshape(FILE_BLOCKS, BLOCK_TOKENS, KEY_VALUE_HEADS, HEAD_WIDTH)
    value_block_rows = values.reshape(FILE_BLOCKS, BLOCK_TOKENS, KEY_VALUE_HEADS, HEAD_WIDTH)
    column = jnp.arange((LISTED_ENTRIES + 1) * BLOCK_TOKENS, dtype=jnp.int32)
    query_row = jnp.arange(BLOCK_TOKENS, dtype=jnp.int32)
    key_block = column // BLOCK_TOKENS

    def one_block(block_index):
        owner_dev = block_index // blocks_per_dev
        picked = choose[block_index]
        source = picked // CAP
        entry_slot = picked % CAP
        local_block = fetch_list[owner_dev, source, entry_slot]
        listed_entries = jnp.concatenate([block_index[None].astype(jnp.int32), (source * blocks_per_dev + local_block).astype(jnp.int32)])
        selected_keys = key_block_rows[listed_entries].reshape((LISTED_ENTRIES + 1) * BLOCK_TOKENS, KEY_VALUE_HEADS, HEAD_WIDTH).astype(jnp.float32)
        selected_values = value_block_rows[listed_entries].reshape((LISTED_ENTRIES + 1) * BLOCK_TOKENS, KEY_VALUE_HEADS, HEAD_WIDTH).astype(jnp.float32)
        query_part = query_block_rows[block_index].astype(jnp.float32)
        scores = jnp.einsum('qhgd,khd->hgqk', query_part, selected_keys) * scaling
        own_ok = (key_block == 0)[None, :] & (column[None, :] <= query_row[:, None])
        import_ok = ((key_block >= 1) & (key_block <= live[block_index]))[None, :]
        allowed = own_ok | import_ok
        scores = jnp.where(allowed[None, None], scores, -jnp.inf)
        highest = lax.optimization_barrier(jnp.max(scores, axis=-1, keepdims=True))
        weights = jnp.exp(scores - highest)
        totals = lax.optimization_barrier(jnp.sum(weights, axis=-1))
        rounded = lax.optimization_barrier(weights.astype(jnp.bfloat16)).astype(jnp.float32)
        mixed = jnp.einsum('hgqk,khd->qhgd', rounded, selected_values)
        result = mixed / jnp.transpose(totals, (2, 0, 1))[..., None]
        return result.astype(jnp.bfloat16).reshape(BLOCK_TOKENS, QUERY_HEADS * HEAD_WIDTH)
    outputs = lax.map(one_block, jnp.arange(FILE_BLOCKS, dtype=jnp.int32))
    return outputs.reshape(CONTEXT_TOKENS, QUERY_HEADS * HEAD_WIDTH)
```

```python
import functools
import math

import jax
import jax.numpy as jnp
from jax import lax
from jax.experimental import pallas as pl
from jax.experimental.pallas import tpu as pltpu
from jax.sharding import PartitionSpec as P

HEAD_WIDTH = 128
BLOCK_TOKENS = 64
LISTED_ENTRIES = 16
CAP = 2
STEP_BLOCKS = 4
MASKED = -1e30
NEAR = 4
ATTEND_FLOPS = 6 * 10**9
ROW_ORDER = (1, 2, 3)
VMEM_BYTES = 60 * 2**20
ANY = pl.BlockSpec(memory_space=pl.ANY)
SMEM = pl.BlockSpec(memory_space=pltpu.SMEM)


def entries(rows_of):
    return [(a, m) for a in range(rows_of) for m in range(NEAR) if (a, m) != (0, 0)]


def count_of(form, rows_of):
    return {"shard": 1, "place": NEAR, "row": rows_of}[form]


def lengths_of(form, rows_of):
    if form == "place":
        return [rows_of - (m == 0) for m in range(NEAR)]
    return [NEAR - (a == 0) for a in range(rows_of)]


def entry_of(form, arrays, ahead, m):
    if form == "place":
        return arrays[m].at[ahead - (m == 0)]
    return arrays[ahead].at[m - (ahead == 0)]


def pick_kernel(shape, place, wanted, keys, values, *refs):
    planes, n_seq, form, tokens, local_heads, first, group_heads, after_n = shape
    rows_of, near = n_seq // NEAR, NEAR
    others, outs = refs[: planes - 1], refs[planes - 1 + after_n : -3]
    shard, load_sems, sems = refs[-3:]
    seq, head = place[0], place[1]
    lanes = group_heads * HEAD_WIDTH
    column = pl.multiple_of((head * local_heads + first) * HEAD_WIDTH, HEAD_WIDTH)

    def part(plane):
        return pl.ds(pl.multiple_of(plane * tokens, tokens), tokens)

    loads = []
    for which, source in enumerate((keys, values)):
        loads.append((source.at[:, pl.ds(column, lanes)], shard.at[which, part(head)]))
    for turn in range(1, planes):
        loads.append((others[turn - 1], shard.at[:, part(lax.rem(head + turn, planes))]))
    loads = [pltpu.make_async_copy(*ends, load_sems.at[i]) for i, ends in enumerate(loads)]
    for copy in loads:
        copy.start()
    for copy in loads:
        copy.wait()

    def each(h, dest, out, act):
        columns = slice(h * HEAD_WIDTH, (h + 1) * HEAD_WIDTH)
        for entry in range(CAP):
            row = pl.multiple_of(wanted[dest, entry] * BLOCK_TOKENS, BLOCK_TOKENS)
            source = shard.at[:, pl.ds(row, BLOCK_TOKENS), columns]
            into = out.at[:, pl.ds(entry * BLOCK_TOKENS, BLOCK_TOKENS)]
            act(pltpu.make_async_copy(source, into, sems.at[h, dest, entry]))

    def all_of(act):
        for h in range(group_heads):
            if form == "shard":

                @pl.loop(seq + 1, n_seq)
                def _(dest):
                    each(h, dest, outs[h].at[dest], act)

            else:
                mine = outs[h * len(outs) // group_heads :]
                for ahead, m in entries(rows_of):
                    dest = (seq // near + ahead) * near + jnp.bitwise_xor(seq % near, m)

                    @pl.when((dest > seq) & (dest < n_seq))
                    def _():
                        each(h, dest, entry_of(form, mine, ahead, m), act)

    all_of(lambda copy: copy.start())
    all_of(lambda copy: copy.wait())


def regroup_kernel(shape, place, *refs):
    n_seq, form, into, back = shape
    rows_of = n_seq // NEAR
    n_in, n_out = count_of(form, rows_of), count_of(into, rows_of)
    ins, outs, bufs = refs[:n_in], refs[n_in : n_in + n_out], refs[n_in + n_out : -2]
    load_sems, sems = refs[-2:]
    row = place[0] // NEAR
    loads = [pltpu.make_async_copy(ins[i], bufs[i], load_sems.at[i]) for i in range(n_in)]

    def stores(act):
        for ahead, m in entries(rows_of):

            @pl.when((row - ahead >= 0) if back else (row + ahead < rows_of))
            def _():
                ends = entry_of(form, bufs, ahead, m), entry_of(into, outs, ahead, m)
                act(pltpu.make_async_copy(*ends, sems.at[ahead, m]))

    for copy in loads:
        copy.start()
    for copy in loads:
        copy.wait()
    stores(lambda copy: copy.start())
    stores(lambda copy: copy.wait())


def attend_scratch(n_seq, tokens, group_heads, repeat):
    blocks_here = tokens // BLOCK_TOKENS
    rows, columns = repeat * BLOCK_TOKENS, STEP_BLOCKS * BLOCK_TOKENS
    steps = LISTED_ENTRIES // STEP_BLOCKS + 1
    units = group_heads * blocks_here * steps + 4
    return [
        pltpu.VMEM((group_heads, tokens, repeat * HEAD_WIDTH), jnp.bfloat16),
        pltpu.VMEM(
            (group_heads, 2, (n_seq * CAP + blocks_here) * BLOCK_TOKENS, HEAD_WIDTH), jnp.bfloat16
        ),
        pltpu.VMEM((group_heads, tokens, repeat * HEAD_WIDTH), jnp.bfloat16),
        pltpu.VMEM((rows, columns), jnp.float32),
        pltpu.VMEM((rows, columns), jnp.bfloat16),
        pltpu.VMEM((rows, HEAD_WIDTH), jnp.float32),
        pltpu.VMEM((rows, HEAD_WIDTH), jnp.float32),
        pltpu.VMEM((rows, HEAD_WIDTH), jnp.float32),
        pltpu.VMEM((rows, HEAD_WIDTH), jnp.float32),
        pltpu.SMEM((units, 4), jnp.int32),
        pltpu.SMEM((units, STEP_BLOCKS), jnp.int32),
        pltpu.SemaphoreType.DMA((group_heads, 3)),
        pltpu.SemaphoreType.DMA((n_seq, group_heads)),
        pltpu.SemaphoreType.DMA((group_heads, blocks_here)),
    ]


def attend_kernel(shape, place, choose, live, queries, keys, values, *refs):
    n_seq, n_head, local_heads, repeat, jobs, aliased = shape
    group_heads = len(jobs)
    pieces = []
    for _, plane, _, form in jobs:
        count = count_of(form, n_seq // NEAR)
        pieces.append((form, refs[:count] if form != "shard" else [refs[0].at[plane]]))
        refs = refs[count:]
    refs = refs[1 if aliased else 0 :]
    out, q_buf, kv_buf, o_buf, scores, weights, acc, top, total, shrink = refs[:10]
    units, taken, sems, piece_sems, out_sems = refs[10:]
    tokens = q_buf.shape[1]
    blocks_here = tokens // BLOCK_TOKENS
    seq, head = place[0], place[1]
    first_block = head * blocks_here
    slots = n_seq * CAP
    q_lanes = repeat * HEAD_WIDTH
    piece_rows = CAP * BLOCK_TOKENS
    own_rows = pl.ds(slots * BLOCK_TOKENS, tokens)
    columns = STEP_BLOCKS * BLOCK_TOKENS
    rows = repeat * BLOCK_TOKENS

    def kv_head(h):
        whose, plane, at, _ = jobs[h]
        return (lax.rem(head + plane, n_head) if whose == "turn" else plane) * local_heads + at

    q_heads = [kv_head(h) for h in range(group_heads)]

    loads = []
    for h in range(group_heads):
        q_cols = pl.ds(pl.multiple_of(q_heads[h] * q_lanes, HEAD_WIDTH), q_lanes)
        kv_cols = pl.ds(pl.multiple_of(q_heads[h] * HEAD_WIDTH, HEAD_WIDTH), HEAD_WIDTH)
        loads += [
            pltpu.make_async_copy(queries.at[:, q_cols], q_buf.at[h], sems.at[h, 0]),
            pltpu.make_async_copy(keys.at[:, kv_cols], kv_buf.at[h, 0, own_rows], sems.at[h, 1]),
            pltpu.make_async_copy(values.at[:, kv_cols], kv_buf.at[h, 1, own_rows], sems.at[h, 2]),
        ]

    def piece_do(h, source, piece, act):
        into = pl.ds(pl.multiple_of(source * piece_rows, piece_rows), piece_rows)
        act(pltpu.make_async_copy(piece, kv_buf.at[h, :, into], piece_sems.at[source, h]))

    def pieces_do(act):
        for h, (form, arrays) in enumerate(pieces):
            if form == "shard":

                @pl.loop(0, seq)
                def _(source):
                    piece_do(h, source, arrays[0].at[source], act)

            else:
                for behind, m in entries(n_seq // NEAR):
                    source = (seq // NEAR - behind) * NEAR + jnp.bitwise_xor(seq % NEAR, m)

                    @pl.when((source >= 0) & (source < seq))
                    def _():
                        piece_do(h, source, entry_of(form, arrays, behind, m), act)

    for copy in loads:
        copy.start()
    pieces_do(lambda copy: copy.start())

    def put(unit, h, block, at, last):
        units[unit, 0] = h
        units[unit, 1] = block
        units[unit, 2] = at
        units[unit, 3] = last
        count = live[first_block + block]
        for i in range(STEP_BLOCKS):
            entry = at * STEP_BLOCKS + i
            slot = choose[first_block + block, jnp.clip(entry - 1, 0, LISTED_ENTRIES - 1)]
            dead = (entry == 0) | (entry > count)
            taken[unit, i] = jnp.where(dead, slots + block, slot) * BLOCK_TOKENS

    put(0, 0, 0, 0, 0)
    put(1, 0, 0, 0, 0)

    def put_block(i, at_unit):
        h, block = i // blocks_here, i % blocks_here
        steps = (live[first_block + block] + STEP_BLOCKS) // STEP_BLOCKS

        @pl.loop(0, steps)
        def _(at):
            put(at_unit + at, h, block, at, jnp.where(at == steps - 1, 1, 0))

        return at_unit + steps

    last_unit = lax.fori_loop(0, group_heads * blocks_here, put_block, jnp.int32(2))
    put(last_unit, 0, 0, 0, 0)
    put(last_unit + 1, 0, 0, 0, 0)

    scores[...] = jnp.zeros_like(scores)
    weights[...] = jnp.zeros_like(weights)
    for buf in (acc, top, total, shrink):
        buf[...] = jnp.zeros_like(buf)

    for copy in loads:
        copy.wait()
    pieces_do(lambda copy: copy.wait())

    factor = math.log2(math.e) / math.sqrt(HEAD_WIDTH)
    column = lax.broadcasted_iota(jnp.int32, (BLOCK_TOKENS, columns), 1)
    row = lax.broadcasted_iota(jnp.int32, (BLOCK_TOKENS, columns), 0)

    def block_rows(block):
        return pl.ds(pl.multiple_of(block * BLOCK_TOKENS, BLOCK_TOKENS), BLOCK_TOKENS)

    def out_copy(h, block):
        at = block_rows(block)
        q_head = q_heads[0]
        for i in range(1, group_heads):
            q_head = jnp.where(h == i, q_heads[i], q_head)
        q_cols = pl.ds(pl.multiple_of(q_head * q_lanes, HEAD_WIDTH), q_lanes)
        return pltpu.make_async_copy(o_buf.at[h, at], out.at[at, q_cols], out_sems.at[h, block])

    def gathered(unit, which):
        h = units[unit, 0]
        parts = []
        for i in range(STEP_BLOCKS):
            at = pl.ds(pl.multiple_of(taken[unit, i], BLOCK_TOKENS), BLOCK_TOKENS)
            parts.append(kv_buf[h, which, at, :])
        return jnp.concatenate(parts, axis=0)

    def turn(unit, carry):
        oldest = unit - 2
        mixed = jnp.dot(weights[...], gathered(oldest, 1), preferred_element_type=jnp.float32)
        mixed = acc[...] * shrink[...] + mixed
        acc[...] = mixed
        result = (mixed * (1.0 / total[...])).astype(jnp.bfloat16)
        h, at = units[oldest, 0], block_rows(units[oldest, 1])
        for r in range(repeat):
            o_buf[h, at, r * HEAD_WIDTH : (r + 1) * HEAD_WIDTH] = result[
                r * BLOCK_TOKENS : (r + 1) * BLOCK_TOKENS
            ]

        before = unit - 1
        at_step = units[before, 2]
        count = live[first_block + units[before, 1]]
        limit = (count + 1 - at_step * STEP_BLOCKS) * BLOCK_TOKENS
        reach = jnp.where(at_step == 0, 0, columns)
        allowed = (column < limit) & ((column >= BLOCK_TOKENS) | (column <= row + reach))
        old = jnp.where(at_step == 0, MASKED, top[...])
        kept = jnp.where(
            allowed[None], scores[...].reshape(repeat, BLOCK_TOKENS, columns), MASKED
        ).reshape(rows, columns)
        high = jnp.maximum(jnp.max(kept, axis=-1, keepdims=True), old)
        fade = jnp.exp2((old - high) * factor)
        parts = [
            jnp.exp2((kept[:, i : i + HEAD_WIDTH] - high) * factor)
            for i in range(0, columns, HEAD_WIDTH)
        ]
        sums = jnp.sum(functools.reduce(jnp.add, parts), axis=-1, keepdims=True)
        for i, part in enumerate(parts):
            weights[:, i * HEAD_WIDTH : (i + 1) * HEAD_WIDTH] = part.astype(jnp.bfloat16)
        top[...] = high
        shrink[...] = fade
        total[...] = total[...] * fade + sums

        h, at = units[unit, 0], block_rows(units[unit, 1])
        q = jnp.concatenate(
            [q_buf[h, at, r * HEAD_WIDTH : (r + 1) * HEAD_WIDTH] for r in range(repeat)], axis=0
        )
        scores[...] = lax.dot_general(
            q, gathered(unit, 0), (((1,), (1,)), ((), ())), preferred_element_type=jnp.float32
        )

        @pl.when(units[oldest, 3] == 1)
        def _():
            out_copy(units[oldest, 0], units[oldest, 1]).start()

        return carry

    lax.fori_loop(2, last_unit + 2, turn, 0)

    for h in range(group_heads):

        @pl.loop(0, blocks_here)
        def _(block):
            out_copy(h, block).wait()


def body(queries, keys, values, fetch_list, choose, live, *, n_seq, n_head):
    tokens, q_width = queries.shape
    kv_heads = keys.shape[1] // HEAD_WIDTH
    repeat = q_width // HEAD_WIDTH // kv_heads
    local_heads = kv_heads // n_head
    rows_of = n_seq // NEAR
    seq, head = lax.axis_index("seq"), lax.axis_index("head")
    wanted = lax.dynamic_index_in_dim(fetch_list, seq, 1, keepdims=False)
    place = jnp.stack([seq, head]).astype(jnp.int32)

    def piece(*lead):
        return jax.ShapeDtypeStruct(lead + (2, CAP * BLOCK_TOKENS, HEAD_WIDTH), jnp.bfloat16)

    def exchange(first, heads):
        others = []
        for turn in range(1, n_head):
            theirs = lax.rem(head + n_head - turn, n_head) * local_heads + first
            part = jnp.stack(
                [
                    lax.dynamic_slice_in_dim(x, theirs * HEAD_WIDTH, heads * HEAD_WIDTH, axis=1)
                    for x in (keys, values)
                ]
            )
            back = [(h, (h + n_head - turn) % n_head) for h in range(n_head)]
            others.append(lax.ppermute(part, "head", back))
        return others

    def pick(first, heads, form, others, after=()):
        if form == "shard":
            shapes = [piece(n_seq)] * heads
        else:
            shapes = [piece(n) for n in lengths_of(form, rows_of)] * heads
        outs = pl.pallas_call(
            functools.partial(
                pick_kernel,
                (n_head, n_seq, form, tokens, local_heads, first, heads, len(after)),
            ),
            out_shape=shapes,
            in_specs=[SMEM, SMEM] + [ANY] * (2 + len(others) + len(after)),
            out_specs=[ANY] * len(shapes),
            scratch_shapes=[
                pltpu.VMEM((2, n_head * tokens, heads * HEAD_WIDTH), jnp.bfloat16),
                pltpu.SemaphoreType.DMA((1 + n_head,)),
                pltpu.SemaphoreType.DMA((heads, n_seq, CAP)),
            ],
            compiler_params=pltpu.CompilerParams(vmem_limit_bytes=VMEM_BYTES),
            name="pick",
        )(place, wanted, keys, values, *others, *after)
        per_head = len(shapes) // heads
        return [outs[h * per_head : (h + 1) * per_head] for h in range(heads)]

    def regroup(form, into, back, parts):
        return pl.pallas_call(
            functools.partial(regroup_kernel, (n_seq, form, into, back)),
            out_shape=[piece(n) for n in lengths_of(into, rows_of)],
            in_specs=[SMEM] + [ANY] * len(parts),
            out_specs=[ANY] * count_of(into, rows_of),
            scratch_shapes=[pltpu.VMEM(part.shape, part.dtype) for part in parts]
            + [pltpu.SemaphoreType.DMA((len(parts),)), pltpu.SemaphoreType.DMA((rows_of, NEAR))],
            compiler_params=pltpu.CompilerParams(vmem_limit_bytes=VMEM_BYTES),
            name="regroup",
        )(place, *parts)

    def attend(jobs, out):
        aliased = out is not None
        operands = [place, choose, live, queries, keys, values]
        shapes = []
        for whose, plane, at, form, arrays in jobs:
            operands += arrays
            shapes.append((whose, plane, at, form))
        operands += [out] if aliased else []
        return pl.pallas_call(
            functools.partial(
                attend_kernel, (n_seq, n_head, local_heads, repeat, tuple(shapes), aliased)
            ),
            out_shape=jax.ShapeDtypeStruct(queries.shape, queries.dtype),
            in_specs=[SMEM] * 3 + [ANY] * (len(operands) - 3),
            out_specs=ANY,
            scratch_shapes=attend_scratch(n_seq, tokens, len(jobs), repeat),
            input_output_aliases={len(operands) - 1: 0} if aliased else {},
            compiler_params=pltpu.CompilerParams(vmem_limit_bytes=VMEM_BYTES),
            cost_estimate=pl.CostEstimate(
                flops=ATTEND_FLOPS * len(jobs), bytes_accessed=8 * 2**20, transcendentals=0
            ),
            name="attend",
        )(*operands)

    def over_rows(arrays):
        got = [arrays[0]] + [None] * (rows_of - 1)
        for ahead in ROW_ORDER:
            step = ahead * NEAR
            pairs = [(s, s + step) for s in range(n_seq - step)]
            got[ahead] = lax.ppermute(arrays[ahead], "seq", pairs)
        return got

    def in_row(arrays):
        return [arrays[0]] + [
            lax.ppermute(arrays[m], "seq", [(s, s ^ m) for s in range(n_seq)])
            for m in range(1, NEAR)
        ]

    def swap(arrays):
        return [lax.ppermute(x, "head", [(0, 1), (1, 0)]) for x in arrays]

    if n_head != 2 or rows_of != 4 or local_heads != 4:
        out = None
        for at in range(local_heads):
            sends = pick(at, 1, "shard", exchange(at, 1))[0]
            got = lax.all_to_all(sends[0], "seq", split_axis=0, concat_axis=0, tiled=True)
            whole = lax.all_gather(got, "head", axis=0, tiled=False)
            for plane in range(n_head):
                out = attend([("plane", plane, at, "shard", [whole])], out)
        return out

    first, second, rest = exchange(0, 1), exchange(1, 1), exchange(2, local_heads - 2)
    sent = over_rows(pick(0, 1, "row", first)[0])
    parts = in_row(pick(1, 1, "place", second)[0])
    grouped = regroup("place", "row", False, parts)
    imports = [None, ("row", over_rows(grouped))]
    picked = pick(2, local_heads - 2, "place", rest, [grouped[0]])
    imports[0] = ("place", in_row(regroup("row", "place", True, sent)))
    for sends in picked:
        imports.append(("row", over_rows(regroup("place", "row", False, in_row(sends)))))
    turned = [(form, swap(arrays)) for form, arrays in imports]
    out = None
    for at in range(local_heads + 1):
        jobs = []
        if at > 0:
            jobs.append(("turn", 1, at - 1) + turned[at - 1])
        if at < local_heads:
            jobs.append(("turn", 0, at) + imports[at])
        out = attend(jobs, out)
    return out


def solution(mesh):
    placed = (
        P(("seq", "head"), None),
        P(("seq", "head"), None),
        P(("seq", "head"), None),
        P(),
        P("seq", None),
        P("seq"),
    )
    return jax.shard_map(
        functools.partial(body, n_seq=mesh.shape["seq"], n_head=mesh.shape["head"]),
        mesh=mesh,
        in_specs=placed,
        out_specs=P(("seq", "head"), None),
        check_vma=False,
    )
```

```python
import functools
import math

import jax
import jax.numpy as jnp
from jax import lax
from jax.experimental import pallas as pl
from jax.experimental.pallas import tpu as pltpu
from jax.sharding import PartitionSpec as P

HEAD_WIDTH = 128
BLOCK_TOKENS = 64
LISTED_ENTRIES = 16
CAP = 2
STEP_BLOCKS = 4
MASKED = -1e30
NEAR = 4
ATTEND_FLOPS = 6 * 10**9
ROW_ORDER = (1, 2, 3)
PICK_FLOPS = 5 * 10**9
VMEM_BYTES = 63 * 2**20
ANY = pl.BlockSpec(memory_space=pl.ANY)
SMEM = pl.BlockSpec(memory_space=pltpu.SMEM)


def entries(rows_of):
    return [(a, m) for a in range(rows_of) for m in range(NEAR) if (a, m) != (0, 0)]


def count_of(form, rows_of):
    return {"shard": 1, "place": NEAR, "row": rows_of}[form]


def lengths_of(form, rows_of):
    if form == "place":
        return [rows_of - (m == 0) for m in range(NEAR)]
    return [NEAR - (a == 0) for a in range(rows_of)]


def entry_of(form, arrays, ahead, m):
    if form == "place":
        return arrays[m].at[ahead - (m == 0)]
    return arrays[ahead].at[m - (ahead == 0)]


def pick_kernel(shape, place, wanted, keys, values, *refs):
    planes, n_seq, forms, tokens, local_heads, first = shape
    rows_of, near = n_seq // NEAR, NEAR
    group_heads = len(forms)
    others, outs = refs[: planes - 1], refs[planes - 1 : -3]
    shard, load_sems, sems = refs[-3:]
    seq, head = place[0], place[1]
    lanes = group_heads * HEAD_WIDTH
    column = pl.multiple_of((head * local_heads + first) * HEAD_WIDTH, HEAD_WIDTH)

    def part(plane):
        return pl.ds(pl.multiple_of(plane * tokens, tokens), tokens)

    loads = []
    for which, source in enumerate((keys, values)):
        loads.append((source.at[:, pl.ds(column, lanes)], shard.at[which, part(head)]))
    for turn in range(1, planes):
        loads.append((others[turn - 1], shard.at[:, part(lax.rem(head + turn, planes))]))
    loads = [pltpu.make_async_copy(*ends, load_sems.at[i]) for i, ends in enumerate(loads)]
    for copy in loads:
        copy.start()
    for copy in loads:
        copy.wait()

    def each(h, dest, out, act):
        columns = slice(h * HEAD_WIDTH, (h + 1) * HEAD_WIDTH)
        for entry in range(CAP):
            row = pl.multiple_of(wanted[dest, entry] * BLOCK_TOKENS, BLOCK_TOKENS)
            source = shard.at[:, pl.ds(row, BLOCK_TOKENS), columns]
            into = out.at[:, pl.ds(entry * BLOCK_TOKENS, BLOCK_TOKENS)]
            act(pltpu.make_async_copy(source, into, sems.at[h, dest, entry]))

    def all_of(act):
        at = 0
        for h, form in enumerate(forms):
            mine = outs[at : at + count_of(form, rows_of)]
            at += len(mine)
            if form == "shard":

                @pl.loop(seq + 1, n_seq)
                def _(dest):
                    each(h, dest, mine[0].at[dest], act)

            else:
                for ahead, m in entries(rows_of):
                    dest = (seq // near + ahead) * near + jnp.bitwise_xor(seq % near, m)

                    @pl.when((dest > seq) & (dest < n_seq))
                    def _():
                        each(h, dest, entry_of(form, mine, ahead, m), act)

    all_of(lambda copy: copy.start())
    all_of(lambda copy: copy.wait())


def regroup_kernel(shape, place, *refs):
    n_seq, form, into, back, passed = shape
    rows_of = n_seq // NEAR
    n_in, n_out = count_of(form, rows_of), count_of(into, rows_of)
    ins, refs = refs[:n_in], refs[n_in + passed :]
    outs, bufs = refs[:n_out], refs[n_out + passed : -2]
    load_sems, sems = refs[-2:]
    row = place[0] // NEAR
    loads = [pltpu.make_async_copy(ins[i], bufs[i], load_sems.at[i]) for i in range(n_in)]

    def stores(act):
        for ahead, m in entries(rows_of):

            @pl.when((row - ahead >= 0) if back else (row + ahead < rows_of))
            def _():
                ends = entry_of(form, bufs, ahead, m), entry_of(into, outs, ahead, m)
                act(pltpu.make_async_copy(*ends, sems.at[ahead, m]))

    for copy in loads:
        copy.start()
    for copy in loads:
        copy.wait()
    stores(lambda copy: copy.start())
    stores(lambda copy: copy.wait())


def attend_scratch(n_seq, tokens, group_heads, repeat):
    blocks_here = tokens // BLOCK_TOKENS
    rows, columns = repeat * BLOCK_TOKENS, STEP_BLOCKS * BLOCK_TOKENS
    steps = LISTED_ENTRIES // STEP_BLOCKS + 1
    units = group_heads * blocks_here * steps + 4
    return [
        pltpu.VMEM((group_heads, tokens, repeat * HEAD_WIDTH), jnp.bfloat16),
        pltpu.VMEM(
            (group_heads, 2, (n_seq * CAP + blocks_here) * BLOCK_TOKENS, HEAD_WIDTH), jnp.bfloat16
        ),
        pltpu.VMEM((group_heads, tokens, repeat * HEAD_WIDTH), jnp.bfloat16),
        pltpu.VMEM((rows, columns), jnp.float32),
        pltpu.VMEM((rows, columns), jnp.bfloat16),
        pltpu.VMEM((rows, HEAD_WIDTH), jnp.float32),
        pltpu.VMEM((rows, HEAD_WIDTH), jnp.float32),
        pltpu.VMEM((rows, HEAD_WIDTH), jnp.float32),
        pltpu.VMEM((rows, HEAD_WIDTH), jnp.float32),
        pltpu.SMEM((units, 4), jnp.int32),
        pltpu.SMEM((units, STEP_BLOCKS), jnp.int32),
        pltpu.SemaphoreType.DMA((group_heads, 3)),
        pltpu.SemaphoreType.DMA((n_seq, group_heads)),
        pltpu.SemaphoreType.DMA((group_heads, blocks_here)),
    ]


def attend_kernel(shape, place, choose, live, queries, keys, values, *refs):
    n_seq, n_head, local_heads, repeat, jobs, given, outs = shape
    group_heads = len(jobs)
    pieces = []
    for whose, plane, _, form in jobs:
        count = count_of(form, n_seq // NEAR)
        pieces.append((form, refs[:count] if form != "shard" else [refs[0].at[plane if whose == "plane" else 0]]))
        refs = refs[count:]
    out = refs[given]
    refs = refs[given + outs :]
    q_buf, kv_buf, o_buf, scores, weights, acc, top, total, shrink = refs[:9]
    units, taken, sems, piece_sems, out_sems = refs[9:]
    tokens = q_buf.shape[1]
    blocks_here = tokens // BLOCK_TOKENS
    seq, head = place[0], place[1]
    first_block = head * blocks_here
    slots = n_seq * CAP
    q_lanes = repeat * HEAD_WIDTH
    piece_rows = CAP * BLOCK_TOKENS
    own_rows = pl.ds(slots * BLOCK_TOKENS, tokens)
    columns = STEP_BLOCKS * BLOCK_TOKENS
    rows = repeat * BLOCK_TOKENS

    def kv_head(h):
        whose, plane, at, _ = jobs[h]
        return (lax.rem(head + plane, n_head) if whose == "turn" else plane) * local_heads + at

    q_heads = [kv_head(h) for h in range(group_heads)]

    loads = []
    for h in range(group_heads):
        q_cols = pl.ds(pl.multiple_of(q_heads[h] * q_lanes, HEAD_WIDTH), q_lanes)
        kv_cols = pl.ds(pl.multiple_of(q_heads[h] * HEAD_WIDTH, HEAD_WIDTH), HEAD_WIDTH)
        loads += [
            pltpu.make_async_copy(queries.at[:, q_cols], q_buf.at[h], sems.at[h, 0]),
            pltpu.make_async_copy(keys.at[:, kv_cols], kv_buf.at[h, 0, own_rows], sems.at[h, 1]),
            pltpu.make_async_copy(values.at[:, kv_cols], kv_buf.at[h, 1, own_rows], sems.at[h, 2]),
        ]

    def piece_do(h, source, piece, act):
        into = pl.ds(pl.multiple_of(source * piece_rows, piece_rows), piece_rows)
        act(pltpu.make_async_copy(piece, kv_buf.at[h, :, into], piece_sems.at[source, h]))

    def pieces_do(act):
        for h, (form, arrays) in enumerate(pieces):
            if form == "shard":

                @pl.loop(0, seq)
                def _(source):
                    piece_do(h, source, arrays[0].at[source], act)

            else:
                for behind, m in entries(n_seq // NEAR):
                    source = (seq // NEAR - behind) * NEAR + jnp.bitwise_xor(seq % NEAR, m)

                    @pl.when((source >= 0) & (source < seq))
                    def _():
                        piece_do(h, source, entry_of(form, arrays, behind, m), act)

    for copy in loads:
        copy.start()
    pieces_do(lambda copy: copy.start())

    def put(unit, h, block, at, last):
        units[unit, 0] = h
        units[unit, 1] = block
        units[unit, 2] = at
        units[unit, 3] = last
        count = live[first_block + block]
        for i in range(STEP_BLOCKS):
            entry = at * STEP_BLOCKS + i
            slot = choose[first_block + block, jnp.clip(entry - 1, 0, LISTED_ENTRIES - 1)]
            dead = (entry == 0) | (entry > count)
            taken[unit, i] = jnp.where(dead, slots + block, slot) * BLOCK_TOKENS

    put(0, 0, 0, 0, 0)
    put(1, 0, 0, 0, 0)

    def put_block(i, at_unit):
        h, block = i // blocks_here, i % blocks_here
        steps = (live[first_block + block] + STEP_BLOCKS) // STEP_BLOCKS

        @pl.loop(0, steps)
        def _(at):
            put(at_unit + at, h, block, at, jnp.where(at == steps - 1, 1, 0))

        return at_unit + steps

    last_unit = lax.fori_loop(0, group_heads * blocks_here, put_block, jnp.int32(2))
    put(last_unit, 0, 0, 0, 0)
    put(last_unit + 1, 0, 0, 0, 0)

    scores[...] = jnp.zeros_like(scores)
    weights[...] = jnp.zeros_like(weights)
    for buf in (acc, top, total, shrink):
        buf[...] = jnp.zeros_like(buf)

    for copy in loads:
        copy.wait()
    pieces_do(lambda copy: copy.wait())

    factor = math.log2(math.e) / math.sqrt(HEAD_WIDTH)
    column = lax.broadcasted_iota(jnp.int32, (BLOCK_TOKENS, columns), 1)
    row = lax.broadcasted_iota(jnp.int32, (BLOCK_TOKENS, columns), 0)

    def block_rows(block):
        return pl.ds(pl.multiple_of(block * BLOCK_TOKENS, BLOCK_TOKENS), BLOCK_TOKENS)

    def out_copy(h, block):
        at = block_rows(block)
        q_head = q_heads[0]
        for i in range(1, group_heads):
            q_head = jnp.where(h == i, q_heads[i], q_head)
        q_cols = pl.ds(pl.multiple_of(q_head * q_lanes, HEAD_WIDTH), q_lanes)
        return pltpu.make_async_copy(o_buf.at[h, at], out.at[at, q_cols], out_sems.at[h, block])

    def gathered(unit, which):
        h = units[unit, 0]
        parts = []
        for i in range(STEP_BLOCKS):
            at = pl.ds(pl.multiple_of(taken[unit, i], BLOCK_TOKENS), BLOCK_TOKENS)
            parts.append(kv_buf[h, which, at, :])
        return jnp.concatenate(parts, axis=0)

    def turn(unit, carry):
        oldest = unit - 2
        mixed = jnp.dot(weights[...], gathered(oldest, 1), preferred_element_type=jnp.float32)
        mixed = acc[...] * shrink[...] + mixed
        acc[...] = mixed
        result = (mixed * (1.0 / total[...])).astype(jnp.bfloat16)
        h, at = units[oldest, 0], block_rows(units[oldest, 1])
        for r in range(repeat):
            o_buf[h, at, r * HEAD_WIDTH : (r + 1) * HEAD_WIDTH] = result[
                r * BLOCK_TOKENS : (r + 1) * BLOCK_TOKENS
            ]

        before = unit - 1
        at_step = units[before, 2]
        count = live[first_block + units[before, 1]]
        limit = (count + 1 - at_step * STEP_BLOCKS) * BLOCK_TOKENS
        reach = jnp.where(at_step == 0, 0, columns)
        allowed = (column < limit) & ((column >= BLOCK_TOKENS) | (column <= row + reach))
        old = jnp.where(at_step == 0, MASKED, top[...])
        kept = jnp.where(
            allowed[None], scores[...].reshape(repeat, BLOCK_TOKENS, columns), MASKED
        ).reshape(rows, columns)
        high = jnp.maximum(jnp.max(kept, axis=-1, keepdims=True), old)
        fade = jnp.exp2((old - high) * factor)
        parts = [
            jnp.exp2((kept[:, i : i + HEAD_WIDTH] - high) * factor)
            for i in range(0, columns, HEAD_WIDTH)
        ]
        sums = jnp.sum(functools.reduce(jnp.add, parts), axis=-1, keepdims=True)
        for i, part in enumerate(parts):
            weights[:, i * HEAD_WIDTH : (i + 1) * HEAD_WIDTH] = part.astype(jnp.bfloat16)
        top[...] = high
        shrink[...] = fade
        total[...] = total[...] * fade + sums

        h, at = units[unit, 0], block_rows(units[unit, 1])
        q = jnp.concatenate(
            [q_buf[h, at, r * HEAD_WIDTH : (r + 1) * HEAD_WIDTH] for r in range(repeat)], axis=0
        )
        scores[...] = lax.dot_general(
            q, gathered(unit, 0), (((1,), (1,)), ((), ())), preferred_element_type=jnp.float32
        )

        @pl.when(units[oldest, 3] == 1)
        def _():
            out_copy(units[oldest, 0], units[oldest, 1]).start()

        return carry

    lax.fori_loop(2, last_unit + 2, turn, 0)

    for h in range(group_heads):

        @pl.loop(0, blocks_here)
        def _(block):
            out_copy(h, block).wait()


def body(queries, keys, values, fetch_list, choose, live, *, n_seq, n_head):
    tokens, q_width = queries.shape
    kv_heads = keys.shape[1] // HEAD_WIDTH
    repeat = q_width // HEAD_WIDTH // kv_heads
    local_heads = kv_heads // n_head
    rows_of = n_seq // NEAR
    seq, head = lax.axis_index("seq"), lax.axis_index("head")
    wanted = lax.dynamic_index_in_dim(fetch_list, seq, 1, keepdims=False)
    place = jnp.stack([seq, head]).astype(jnp.int32)

    def piece(*lead):
        return jax.ShapeDtypeStruct(lead + (2, CAP * BLOCK_TOKENS, HEAD_WIDTH), jnp.bfloat16)

    def exchange(first, heads):
        others = []
        for turn in range(1, n_head):
            theirs = lax.rem(head + n_head - turn, n_head) * local_heads + first
            part = jnp.stack(
                [
                    lax.dynamic_slice_in_dim(x, theirs * HEAD_WIDTH, heads * HEAD_WIDTH, axis=1)
                    for x in (keys, values)
                ]
            )
            back = [(h, (h + n_head - turn) % n_head) for h in range(n_head)]
            with jax.named_scope(f"other_plane_{first}"):
                others.append(lax.ppermute(part, "head", back))
        return others

    def pick(first, forms, others):
        shapes = []
        for form in forms:
            lengths = [n_seq] if form == "shard" else lengths_of(form, rows_of)
            shapes += [piece(n) for n in lengths]
        heads = len(forms)
        outs = list(
            pl.pallas_call(
                functools.partial(pick_kernel, (n_head, n_seq, forms, tokens, local_heads, first)),
                out_shape=shapes,
                in_specs=[SMEM, SMEM] + [ANY] * (2 + len(others)),
                out_specs=[ANY] * len(shapes),
                scratch_shapes=[
                    pltpu.VMEM((2, n_head * tokens, heads * HEAD_WIDTH), jnp.bfloat16),
                    pltpu.SemaphoreType.DMA((1 + n_head,)),
                    pltpu.SemaphoreType.DMA((heads, n_seq, CAP)),
                ],
                compiler_params=pltpu.CompilerParams(vmem_limit_bytes=VMEM_BYTES),
                cost_estimate=pl.CostEstimate(
                    flops=PICK_FLOPS * heads, bytes_accessed=2**20, transcendentals=0
                ),
                name="pick",
            )(place, wanted, keys, values, *others)
        )
        return [[outs.pop(0) for _ in range(count_of(form, rows_of))] for form in forms]

    def regroup(form, into, back, parts, *passed):
        n_in, n_out = len(parts), count_of(into, rows_of)
        shapes = [piece(n) for n in lengths_of(into, rows_of)]
        outs = pl.pallas_call(
            functools.partial(regroup_kernel, (n_seq, form, into, back, len(passed))),
            out_shape=shapes + [jax.ShapeDtypeStruct(x.shape, x.dtype) for x in passed],
            in_specs=[SMEM] + [ANY] * (n_in + len(passed)),
            out_specs=[ANY] * (n_out + len(passed)),
            scratch_shapes=[pltpu.VMEM(part.shape, part.dtype) for part in parts]
            + [pltpu.SemaphoreType.DMA((n_in,)), pltpu.SemaphoreType.DMA((rows_of, NEAR))],
            input_output_aliases={1 + n_in + i: n_out + i for i in range(len(passed))},
            compiler_params=pltpu.CompilerParams(vmem_limit_bytes=VMEM_BYTES),
            name="regroup",
        )(place, *parts, *passed)
        return list(outs[:n_out]), *outs[n_out:]

    def attend(jobs, *passed):
        operands = [place, choose, live, queries, keys, values]
        shapes = []
        for whose, plane, at, form, arrays in jobs:
            operands += arrays
            shapes.append((whose, plane, at, form))
        n = len(operands)
        outs = [queries if x is None else x for x in passed or [None]]
        given = [i for i, x in enumerate(outs) if passed and passed[i] is not None]
        operands += [passed[i] for i in given]
        return pl.pallas_call(
            functools.partial(
                attend_kernel, (n_seq, n_head, local_heads, repeat, tuple(shapes), len(given), len(outs))
            ),
            out_shape=[jax.ShapeDtypeStruct(x.shape, x.dtype) for x in outs],
            in_specs=[SMEM] * 3 + [ANY] * (len(operands) - 3),
            out_specs=[ANY] * len(outs),
            scratch_shapes=attend_scratch(n_seq, tokens, len(jobs), repeat),
            input_output_aliases={n + i: at for i, at in enumerate(given)},
            compiler_params=pltpu.CompilerParams(vmem_limit_bytes=VMEM_BYTES),
            cost_estimate=pl.CostEstimate(
                flops=ATTEND_FLOPS * len(jobs), bytes_accessed=2**20, transcendentals=0
            ),
            name="attend",
        )(*operands)

    def over_rows(arrays, at):
        got = [arrays[0]] + [None] * (rows_of - 1)
        for ahead in ROW_ORDER:
            step = ahead * NEAR
            pairs = [(s, s + step) for s in range(n_seq - step)]
            with jax.named_scope(f"row_{at}_{ahead}"):
                got[ahead] = lax.ppermute(arrays[ahead], "seq", pairs)
        return got

    def in_row(arrays, at):
        got = [arrays[0]]
        for m in range(1, NEAR):
            with jax.named_scope(f"place_{at}_{m}"):
                got.append(lax.ppermute(arrays[m], "seq", [(s, s ^ m) for s in range(n_seq)]))
        return got

    def swap(arrays, at):
        got = []
        for i, array in enumerate(arrays):
            with jax.named_scope(f"swap_{at}_{i}"):
                got.append(lax.ppermute(array, "head", [(0, 1), (1, 0)]))
        return got

    if n_head != 2 or rows_of != 4 or local_heads != 4:
        passed = []
        for at in range(local_heads):
            ((sends,),) = pick(at, ("shard",), exchange(at, 1))
            got = lax.all_to_all(sends, "seq", split_axis=0, concat_axis=0, tiled=True)
            whole = lax.all_gather(got, "head", axis=0, tiled=False)
            for plane in range(n_head):
                passed = attend([("plane", plane, at, "shard", [whole])], *passed)
        return passed[0]

    def direct(at, sends):
        with jax.named_scope(f"shard_{at}"):
            got = lax.all_to_all(sends, "seq", split_axis=0, concat_axis=0, tiled=True)
        return "shard", [got[None]]

    def own(at, imports):
        return ("turn", 0, at) + imports

    def turned(at, imports):
        form, arrays = imports
        return ("turn", 1, at, form, swap(arrays, at))

    others, rest = exchange(0, 1), exchange(1, 3)
    first = direct(0, pick(0, ("shard",), others)[0][0])
    (sends,), (third,), parts = pick(1, ("shard", "shard", "place"), rest)
    second = direct(1, sends)
    first_turned = swap(first[1], 0)
    out, straight = attend([own(0, first)], None, parts[0])
    parts = [straight] + in_row(parts, 3)[1:]
    grouped, third, *first_turned = regroup("place", "row", False, parts, third, *first_turned)
    third = direct(2, third)
    job = ("turn", 1, 0, "shard", first_turned)
    out, *grouped[:-1] = attend([job, own(1, second)], out, *grouped[:-1])
    out, grouped[-1] = attend([turned(1, second), own(2, third)], out, grouped[-1])
    fourth = "row", over_rows(grouped, 3)
    (out,) = attend([turned(2, third), own(3, fourth)], out)
    (out,) = attend([turned(3, fourth)], out)
    return out


def solution(mesh):
    placed = (
        P(("seq", "head"), None),
        P(("seq", "head"), None),
        P(("seq", "head"), None),
        P(),
        P("seq", None),
        P("seq"),
    )
    return jax.shard_map(
        functools.partial(body, n_seq=mesh.shape["seq"], n_head=mesh.shape["head"]),
        mesh=mesh,
        in_specs=placed,
        out_specs=P(("seq", "head"), None),
        check_vma=False,
    )
```

```python
import functools
import math

import jax
import jax.numpy as jnp
from jax import lax
from jax.experimental import pallas as pl
from jax.experimental.pallas import tpu as pltpu
from jax.sharding import PartitionSpec as P

HEAD_WIDTH = 128
BLOCK_TOKENS = 64
LISTED_ENTRIES = 16
CAP = 2
STEP_BLOCKS = 4
MASKED = -1e30
NEAR = 4
ATTEND_FLOPS = 6 * 10**9
ROW_ORDER = (2, 1, 3)
PICK_FLOPS = 5 * 10**9
VMEM_BYTES = 63 * 2**20
ANY = pl.BlockSpec(memory_space=pl.ANY)
SMEM = pl.BlockSpec(memory_space=pltpu.SMEM)


def entries(rows_of):
    return [(a, m) for a in range(rows_of) for m in range(NEAR) if (a, m) != (0, 0)]


def count_of(form, rows_of):
    return {"shard": 1, "place": NEAR, "row": rows_of}[form]


def lengths_of(form, rows_of):
    if form == "place":
        return [rows_of - (m == 0) for m in range(NEAR)]
    return [NEAR - (a == 0) for a in range(rows_of)]


def entry_of(form, arrays, ahead, m):
    if form == "place":
        return arrays[m].at[ahead - (m == 0)]
    return arrays[ahead].at[m - (ahead == 0)]


def pick_kernel(shape, place, wanted, keys, values, *refs):
    planes, n_seq, forms, tokens, local_heads, first = shape
    rows_of, near = n_seq // NEAR, NEAR
    group_heads = len(forms)
    others, outs = refs[: planes - 1], refs[planes - 1 : -3]
    shard, load_sems, sems = refs[-3:]
    seq, head = place[0], place[1]
    lanes = group_heads * HEAD_WIDTH
    column = pl.multiple_of((head * local_heads + first) * HEAD_WIDTH, HEAD_WIDTH)

    def part(plane):
        return pl.ds(pl.multiple_of(plane * tokens, tokens), tokens)

    loads = []
    for which, source in enumerate((keys, values)):
        loads.append((source.at[:, pl.ds(column, lanes)], shard.at[which, part(head)]))
    for turn in range(1, planes):
        loads.append((others[turn - 1], shard.at[:, part(lax.rem(head + turn, planes))]))
    loads = [pltpu.make_async_copy(*ends, load_sems.at[i]) for i, ends in enumerate(loads)]
    for copy in loads:
        copy.start()
    for copy in loads:
        copy.wait()

    def each(h, dest, out, act):
        columns = slice(h * HEAD_WIDTH, (h + 1) * HEAD_WIDTH)
        for entry in range(CAP):
            row = pl.multiple_of(wanted[dest, entry] * BLOCK_TOKENS, BLOCK_TOKENS)
            source = shard.at[:, pl.ds(row, BLOCK_TOKENS), columns]
            into = out.at[:, pl.ds(entry * BLOCK_TOKENS, BLOCK_TOKENS)]
            act(pltpu.make_async_copy(source, into, sems.at[h, dest, entry]))

    def all_of(act):
        at = 0
        for h, form in enumerate(forms):
            mine = outs[at : at + count_of(form, rows_of)]
            at += len(mine)
            if form == "shard":

                @pl.loop(seq + 1, n_seq)
                def _(dest):
                    each(h, dest, mine[0].at[dest], act)

            else:
                for ahead, m in entries(rows_of):
                    dest = (seq // near + ahead) * near + jnp.bitwise_xor(seq % near, m)

                    @pl.when((dest > seq) & (dest < n_seq))
                    def _():
                        each(h, dest, entry_of(form, mine, ahead, m), act)

    all_of(lambda copy: copy.start())
    all_of(lambda copy: copy.wait())


def regroup_kernel(shape, place, *refs):
    n_seq, form, into, back, passed = shape
    rows_of = n_seq // NEAR
    n_in, n_out = count_of(form, rows_of), count_of(into, rows_of)
    ins, refs = refs[:n_in], refs[n_in + passed :]
    outs, bufs = refs[:n_out], refs[n_out + passed : -2]
    load_sems, sems = refs[-2:]
    row = place[0] // NEAR
    loads = [pltpu.make_async_copy(ins[i], bufs[i], load_sems.at[i]) for i in range(n_in)]

    def stores(act):
        for ahead, m in entries(rows_of):

            @pl.when((row - ahead >= 0) if back else (row + ahead < rows_of))
            def _():
                ends = entry_of(form, bufs, ahead, m), entry_of(into, outs, ahead, m)
                act(pltpu.make_async_copy(*ends, sems.at[ahead, m]))

    for copy in loads:
        copy.start()
    for copy in loads:
        copy.wait()
    stores(lambda copy: copy.start())
    stores(lambda copy: copy.wait())


def attend_scratch(n_seq, tokens, group_heads, repeat):
    blocks_here = tokens // BLOCK_TOKENS
    rows, columns = repeat * BLOCK_TOKENS, STEP_BLOCKS * BLOCK_TOKENS
    steps = LISTED_ENTRIES // STEP_BLOCKS + 1
    units = group_heads * blocks_here * steps + 5
    return [
        pltpu.VMEM((group_heads, tokens, repeat * HEAD_WIDTH), jnp.bfloat16),
        pltpu.VMEM(
            (group_heads, 2, (n_seq * CAP + blocks_here) * BLOCK_TOKENS, HEAD_WIDTH), jnp.bfloat16
        ),
        pltpu.VMEM((group_heads, tokens + BLOCK_TOKENS, repeat * HEAD_WIDTH), jnp.bfloat16),
        pltpu.VMEM((rows, columns), jnp.float32),
        pltpu.VMEM((rows, columns), jnp.float32),
        pltpu.VMEM((rows, columns), jnp.bfloat16),
        pltpu.VMEM((rows, columns), jnp.bfloat16),
        pltpu.VMEM((rows, HEAD_WIDTH), jnp.float32),
        pltpu.VMEM((rows, HEAD_WIDTH), jnp.float32),
        pltpu.VMEM((rows, HEAD_WIDTH), jnp.float32),
        pltpu.VMEM((rows, HEAD_WIDTH), jnp.float32),
        pltpu.SMEM((units, 5), jnp.int32),
        pltpu.SMEM((units, STEP_BLOCKS), jnp.int32),
        pltpu.SemaphoreType.DMA((group_heads, 3)),
        pltpu.SemaphoreType.DMA((n_seq, group_heads)),
        pltpu.SemaphoreType.DMA((group_heads, blocks_here)),
    ]


def attend_kernel(shape, place, choose, live, queries, keys, values, *refs):
    n_seq, n_head, local_heads, repeat, jobs, given, outs = shape
    group_heads = len(jobs)
    pieces = []
    for whose, plane, _, form in jobs:
        count = count_of(form, n_seq // NEAR)
        pieces.append((form, refs[:count] if form != "shard" else [refs[0].at[plane if whose == "plane" else 0]]))
        refs = refs[count:]
    out = refs[given]
    refs = refs[given + outs :]
    q_buf, kv_buf, o_buf = refs[:3]
    scores, weights = refs[3:5], refs[5:7]
    acc, top, total, shrink, units, taken, sems, piece_sems, out_sems = refs[7:]
    tokens = q_buf.shape[1]
    blocks_here = tokens // BLOCK_TOKENS
    seq, head = place[0], place[1]
    first_block = head * blocks_here
    slots = n_seq * CAP
    q_lanes = repeat * HEAD_WIDTH
    piece_rows = CAP * BLOCK_TOKENS
    own_rows = pl.ds(slots * BLOCK_TOKENS, tokens)
    columns = STEP_BLOCKS * BLOCK_TOKENS
    rows = repeat * BLOCK_TOKENS

    def kv_head(h):
        whose, plane, at, _ = jobs[h]
        return (lax.rem(head + plane, n_head) if whose == "turn" else plane) * local_heads + at

    q_heads = [kv_head(h) for h in range(group_heads)]

    loads = []
    for h in range(group_heads):
        q_cols = pl.ds(pl.multiple_of(q_heads[h] * q_lanes, HEAD_WIDTH), q_lanes)
        kv_cols = pl.ds(pl.multiple_of(q_heads[h] * HEAD_WIDTH, HEAD_WIDTH), HEAD_WIDTH)
        loads += [
            pltpu.make_async_copy(queries.at[:, q_cols], q_buf.at[h], sems.at[h, 0]),
            pltpu.make_async_copy(keys.at[:, kv_cols], kv_buf.at[h, 0, own_rows], sems.at[h, 1]),
            pltpu.make_async_copy(values.at[:, kv_cols], kv_buf.at[h, 1, own_rows], sems.at[h, 2]),
        ]

    def piece_do(h, source, piece, act):
        into = pl.ds(pl.multiple_of(source * piece_rows, piece_rows), piece_rows)
        act(pltpu.make_async_copy(piece, kv_buf.at[h, :, into], piece_sems.at[source, h]))

    def pieces_do(act):
        for h, (form, arrays) in enumerate(pieces):
            if form == "shard":

                @pl.loop(0, seq)
                def _(source):
                    piece_do(h, source, arrays[0].at[source], act)

            else:
                for behind, m in entries(n_seq // NEAR):
                    source = (seq // NEAR - behind) * NEAR + jnp.bitwise_xor(seq % NEAR, m)

                    @pl.when((source >= 0) & (source < seq))
                    def _():
                        piece_do(h, source, entry_of(form, arrays, behind, m), act)

    for copy in loads:
        copy.start()
    pieces_do(lambda copy: copy.start())

    def put(unit, h, block, at, last, out_block):
        units[unit, 0] = h
        units[unit, 1] = block
        units[unit, 2] = at
        units[unit, 3] = last
        units[unit, 4] = out_block
        count = live[first_block + block]
        for i in range(STEP_BLOCKS):
            entry = at * STEP_BLOCKS + i
            slot = choose[first_block + block, jnp.clip(entry - 1, 0, LISTED_ENTRIES - 1)]
            dead = (entry == 0) | (entry > count)
            taken[unit, i] = jnp.where(dead, slots + block, slot) * BLOCK_TOKENS

    for fill in range(2):
        put(fill, 0, 0, 0, 0, blocks_here)

    def put_block(i, at_unit):
        h, block = i // blocks_here, i % blocks_here
        steps = (live[first_block + block] + STEP_BLOCKS) // STEP_BLOCKS

        @pl.loop(0, steps)
        def _(at):
            put(at_unit + at, h, block, at, jnp.where(at == steps - 1, 1, 0), block)

        return at_unit + steps

    last_unit = lax.fori_loop(0, group_heads * blocks_here, put_block, jnp.int32(2))
    for fill in range(3):
        put(last_unit + fill, 0, 0, 0, 0, blocks_here)

    for buf in (*scores, *weights, acc, top, total, shrink):
        buf[...] = jnp.zeros_like(buf)

    for copy in loads:
        copy.wait()
    pieces_do(lambda copy: copy.wait())

    factor = math.log2(math.e) / math.sqrt(HEAD_WIDTH)
    column = lax.broadcasted_iota(jnp.int32, (BLOCK_TOKENS, columns), 1)
    row = lax.broadcasted_iota(jnp.int32, (BLOCK_TOKENS, columns), 0)

    def block_rows(block):
        return pl.ds(pl.multiple_of(block * BLOCK_TOKENS, BLOCK_TOKENS), BLOCK_TOKENS)

    def out_copy(h, block):
        at = block_rows(block)
        q_head = q_heads[0]
        for i in range(1, group_heads):
            q_head = jnp.where(h == i, q_heads[i], q_head)
        q_cols = pl.ds(pl.multiple_of(q_head * q_lanes, HEAD_WIDTH), q_lanes)
        return pltpu.make_async_copy(o_buf.at[h, at], out.at[at, q_cols], out_sems.at[h, block])

    def gathered(unit, which):
        h = units[unit, 0]
        parts = []
        for i in range(STEP_BLOCKS):
            at = pl.ds(pl.multiple_of(taken[unit, i], BLOCK_TOKENS), BLOCK_TOKENS)
            parts.append(kv_buf[h, which, at, :])
        return jnp.concatenate(parts, axis=0)

    def turn(unit, now):
        oldest = unit - 2
        mixed = jnp.dot(weights[now][...], gathered(oldest, 1), preferred_element_type=jnp.float32)
        mixed = acc[...] * shrink[...] + mixed
        acc[...] = mixed
        result = (mixed * (1.0 / total[...])).astype(jnp.bfloat16)
        h, at = units[oldest, 0], block_rows(units[oldest, 4])
        for r in range(repeat):
            o_buf[h, at, r * HEAD_WIDTH : (r + 1) * HEAD_WIDTH] = result[
                r * BLOCK_TOKENS : (r + 1) * BLOCK_TOKENS
            ]

        before = unit - 1
        at_step = units[before, 2]
        count = live[first_block + units[before, 1]]
        limit = (count + 1 - at_step * STEP_BLOCKS) * BLOCK_TOKENS
        reach = jnp.where(at_step == 0, 0, columns)
        allowed = (column < limit) & ((column >= BLOCK_TOKENS) | (column <= row + reach))
        old = jnp.where(at_step == 0, MASKED, top[...])
        kept = jnp.where(
            allowed[None], scores[1 - now][...].reshape(repeat, BLOCK_TOKENS, columns), MASKED
        ).reshape(rows, columns)
        high = jnp.maximum(jnp.max(kept, axis=-1, keepdims=True), old)
        fade = jnp.exp2((old - high) * factor)
        parts = [
            jnp.exp2((kept[:, i : i + HEAD_WIDTH] - high) * factor)
            for i in range(0, columns, HEAD_WIDTH)
        ]
        sums = jnp.sum(functools.reduce(jnp.add, parts), axis=-1, keepdims=True)
        for i, part in enumerate(parts):
            weights[1 - now][:, i * HEAD_WIDTH : (i + 1) * HEAD_WIDTH] = part.astype(jnp.bfloat16)
        top[...] = high
        shrink[...] = fade
        total[...] = total[...] * fade + sums

        h, at = units[unit, 0], block_rows(units[unit, 1])
        q = jnp.concatenate(
            [q_buf[h, at, r * HEAD_WIDTH : (r + 1) * HEAD_WIDTH] for r in range(repeat)], axis=0
        )
        scores[now][...] = lax.dot_general(
            q, gathered(unit, 0), (((1,), (1,)), ((), ())), preferred_element_type=jnp.float32
        )

    def send(unit):
        @pl.when(units[unit, 3] == 1)
        def _():
            out_copy(units[unit, 0], units[unit, 1]).start()

    def two_turns(i, carry):
        unit = 2 * i
        turn(unit, 0)
        turn(unit + 1, 1)
        send(unit - 2)
        send(unit - 1)
        return carry

    lax.fori_loop(1, (last_unit + 3) // 2, two_turns, 0)

    for h in range(group_heads):

        @pl.loop(0, blocks_here)
        def _(block):
            out_copy(h, block).wait()


def body(queries, keys, values, fetch_list, choose, live, *, n_seq, n_head):
    tokens, q_width = queries.shape
    kv_heads = keys.shape[1] // HEAD_WIDTH
    repeat = q_width // HEAD_WIDTH // kv_heads
    local_heads = kv_heads // n_head
    rows_of = n_seq // NEAR
    seq, head = lax.axis_index("seq"), lax.axis_index("head")
    wanted = lax.dynamic_index_in_dim(fetch_list, seq, 1, keepdims=False)
    place = jnp.stack([seq, head]).astype(jnp.int32)

    def piece(*lead):
        return jax.ShapeDtypeStruct(lead + (2, CAP * BLOCK_TOKENS, HEAD_WIDTH), jnp.bfloat16)

    def exchange(first, heads):
        others = []
        for turn in range(1, n_head):
            theirs = lax.rem(head + n_head - turn, n_head) * local_heads + first
            part = jnp.stack(
                [
                    lax.dynamic_slice_in_dim(x, theirs * HEAD_WIDTH, heads * HEAD_WIDTH, axis=1)
                    for x in (keys, values)
                ]
            )
            back = [(h, (h + n_head - turn) % n_head) for h in range(n_head)]
            with jax.named_scope(f"other_plane_{first}"):
                others.append(lax.ppermute(part, "head", back))
        return others

    def pick(first, forms, others):
        shapes = []
        for form in forms:
            lengths = [n_seq] if form == "shard" else lengths_of(form, rows_of)
            shapes += [piece(n) for n in lengths]
        heads = len(forms)
        outs = list(
            pl.pallas_call(
                functools.partial(pick_kernel, (n_head, n_seq, forms, tokens, local_heads, first)),
                out_shape=shapes,
                in_specs=[SMEM, SMEM] + [ANY] * (2 + len(others)),
                out_specs=[ANY] * len(shapes),
                scratch_shapes=[
                    pltpu.VMEM((2, n_head * tokens, heads * HEAD_WIDTH), jnp.bfloat16),
                    pltpu.SemaphoreType.DMA((1 + n_head,)),
                    pltpu.SemaphoreType.DMA((heads, n_seq, CAP)),
                ],
                compiler_params=pltpu.CompilerParams(vmem_limit_bytes=VMEM_BYTES),
                cost_estimate=pl.CostEstimate(
                    flops=PICK_FLOPS * heads, bytes_accessed=2**20, transcendentals=0
                ),
                name="pick",
            )(place, wanted, keys, values, *others)
        )
        return [[outs.pop(0) for _ in range(count_of(form, rows_of))] for form in forms]

    def regroup(form, into, back, parts, *passed):
        n_in, n_out = len(parts), count_of(into, rows_of)
        shapes = [piece(n) for n in lengths_of(into, rows_of)]
        outs = pl.pallas_call(
            functools.partial(regroup_kernel, (n_seq, form, into, back, len(passed))),
            out_shape=shapes + [jax.ShapeDtypeStruct(x.shape, x.dtype) for x in passed],
            in_specs=[SMEM] + [ANY] * (n_in + len(passed)),
            out_specs=[ANY] * (n_out + len(passed)),
            scratch_shapes=[pltpu.VMEM(part.shape, part.dtype) for part in parts]
            + [pltpu.SemaphoreType.DMA((n_in,)), pltpu.SemaphoreType.DMA((rows_of, NEAR))],
            input_output_aliases={1 + n_in + i: n_out + i for i in range(len(passed))},
            compiler_params=pltpu.CompilerParams(vmem_limit_bytes=VMEM_BYTES),
            name="regroup",
        )(place, *parts, *passed)
        return list(outs[:n_out]), *outs[n_out:]

    def attend(jobs, *passed):
        operands = [place, choose, live, queries, keys, values]
        shapes = []
        for whose, plane, at, form, arrays in jobs:
            operands += arrays
            shapes.append((whose, plane, at, form))
        n = len(operands)
        outs = [queries if x is None else x for x in passed or [None]]
        given = [i for i, x in enumerate(outs) if passed and passed[i] is not None]
        operands += [passed[i] for i in given]
        return pl.pallas_call(
            functools.partial(
                attend_kernel, (n_seq, n_head, local_heads, repeat, tuple(shapes), len(given), len(outs))
            ),
            out_shape=[jax.ShapeDtypeStruct(x.shape, x.dtype) for x in outs],
            in_specs=[SMEM] * 3 + [ANY] * (len(operands) - 3),
            out_specs=[ANY] * len(outs),
            scratch_shapes=attend_scratch(n_seq, tokens, len(jobs), repeat),
            input_output_aliases={n + i: at for i, at in enumerate(given)},
            compiler_params=pltpu.CompilerParams(vmem_limit_bytes=VMEM_BYTES),
            cost_estimate=pl.CostEstimate(
                flops=ATTEND_FLOPS * len(jobs), bytes_accessed=2**20, transcendentals=0
            ),
            name="attend",
        )(*operands)

    def over_rows(arrays, at):
        got = [arrays[0]] + [None] * (rows_of - 1)
        for ahead in ROW_ORDER:
            if arrays[ahead] is None:
                continue
            step = ahead * NEAR
            pairs = [(s, s + step) for s in range(n_seq - step)]
            with jax.named_scope(f"row_{at}_{ahead}"):
                got[ahead] = lax.ppermute(arrays[ahead], "seq", pairs)
        return got

    def in_row(arrays, at):
        got = [arrays[0]]
        for m in range(1, NEAR):
            with jax.named_scope(f"place_{at}_{m}"):
                got.append(lax.ppermute(arrays[m], "seq", [(s, s ^ m) for s in range(n_seq)]))
        return got

    def swap(arrays, at):
        got = []
        for i, array in enumerate(arrays):
            with jax.named_scope(f"swap_{at}_{i}"):
                got.append(lax.ppermute(array, "head", [(0, 1), (1, 0)]))
        return got

    if n_head != 2 or rows_of != 4 or local_heads != 4:
        passed = []
        for at in range(local_heads):
            ((sends,),) = pick(at, ("shard",), exchange(at, 1))
            got = lax.all_to_all(sends, "seq", split_axis=0, concat_axis=0, tiled=True)
            whole = lax.all_gather(got, "head", axis=0, tiled=False)
            for plane in range(n_head):
                passed = attend([("plane", plane, at, "shard", [whole])], *passed)
        return passed[0]

    def direct(at, sends):
        with jax.named_scope(f"shard_{at}"):
            got = lax.all_to_all(sends, "seq", split_axis=0, concat_axis=0, tiled=True)
        return "shard", [got[None]]

    def own(at, imports):
        return ("turn", 0, at) + imports

    def turned(at, imports):
        form, arrays = imports
        return ("turn", 1, at, form, swap(arrays, at))

    others, rest = exchange(0, 1), exchange(1, 3)
    first = direct(0, pick(0, ("shard",), others)[0][0])
    (sends,), (third,), parts = pick(1, ("shard", "shard", "place"), rest)
    second = direct(1, sends)
    first_turned = swap(first[1], 0)
    out, straight = attend([own(0, first)], None, parts[0])
    parts = [straight] + in_row(parts, 3)[1:]
    grouped, third, *first_turned = regroup("place", "row", False, parts, third, *first_turned)
    third = direct(2, third)
    job = ("turn", 1, 0, "shard", first_turned)
    out, *grouped[:-1] = attend([job, own(1, second)], out, *grouped[:-1])
    ends = [(i, i ^ 1) for i in range(NEAR * n_head)]
    with jax.named_scope("swap_far"):
        twin = lax.ppermute(grouped[-1], ("seq", "head"), ends)
    out, grouped[-1], twin = attend([turned(1, second), own(2, third)], out, grouped[-1], twin)
    fourth = over_rows(grouped, 3)
    twin = over_rows([None] * (rows_of - 1) + [twin], 4)[-1]
    (out,) = attend([turned(2, third), own(3, ("row", fourth))], out)
    (out,) = attend([("turn", 1, 3, "row", swap(fourth[:-1], 3) + [twin])], out)
    return out


def solution(mesh):
    placed = (
        P(("seq", "head"), None),
        P(("seq", "head"), None),
        P(("seq", "head"), None),
        P(),
        P("seq", None),
        P("seq"),
    )
    return jax.shard_map(
        functools.partial(body, n_seq=mesh.shape["seq"], n_head=mesh.shape["head"]),
        mesh=mesh,
        in_specs=placed,
        out_specs=P(("seq", "head"), None),
        check_vma=False,
    )
```

```python
import functools
import math

import jax
import jax.numpy as jnp
from jax import lax
from jax.experimental import pallas as pl
from jax.experimental.pallas import tpu as pltpu
from jax.sharding import PartitionSpec as P

HEAD_WIDTH = 128
BLOCK_TOKENS = 64
LISTED_ENTRIES = 16
CAP = 2
STEP_BLOCKS = 4
MASKED = -1e30
NEAR = 4
ATTEND_FLOPS = 10 * 10**9
ROW_ORDER = (2, 1, 3)
PICK_FLOPS = 5 * 10**9
VMEM_BYTES = 63 * 2**20
ANY = pl.BlockSpec(memory_space=pl.ANY)
SMEM = pl.BlockSpec(memory_space=pltpu.SMEM)


def entries(rows_of):
    return [(a, m) for a in range(rows_of) for m in range(NEAR) if (a, m) != (0, 0)]


def count_of(form, rows_of):
    return {"shard": 1, "place": NEAR, "row": rows_of}[form]


def lengths_of(form, rows_of):
    if form == "place":
        return [rows_of - (m == 0) for m in range(NEAR)]
    return [NEAR - (a == 0) for a in range(rows_of)]


def entry_of(form, arrays, ahead, m):
    if form == "place":
        return arrays[m].at[ahead - (m == 0)]
    return arrays[ahead].at[m - (ahead == 0)]


def pick_kernel(shape, place, wanted, keys, values, *refs):
    planes, n_seq, forms, tokens, local_heads, first = shape
    rows_of, near = n_seq // NEAR, NEAR
    group_heads = len(forms)
    others, outs = refs[: planes - 1], refs[planes - 1 : -3]
    shard, load_sems, sems = refs[-3:]
    seq, head = place[0], place[1]
    lanes = group_heads * HEAD_WIDTH
    column = pl.multiple_of((head * local_heads + first) * HEAD_WIDTH, HEAD_WIDTH)

    def part(plane):
        return pl.ds(pl.multiple_of(plane * tokens, tokens), tokens)

    loads = []
    for which, source in enumerate((keys, values)):
        loads.append((source.at[:, pl.ds(column, lanes)], shard.at[which, part(head)]))
    for turn in range(1, planes):
        loads.append((others[turn - 1], shard.at[:, part(lax.rem(head + turn, planes))]))
    loads = [pltpu.make_async_copy(*ends, load_sems.at[i]) for i, ends in enumerate(loads)]
    for copy in loads:
        copy.start()
    for copy in loads:
        copy.wait()

    def each(h, dest, out, act):
        columns = slice(h * HEAD_WIDTH, (h + 1) * HEAD_WIDTH)
        for entry in range(CAP):
            row = pl.multiple_of(wanted[dest, entry] * BLOCK_TOKENS, BLOCK_TOKENS)
            source = shard.at[:, pl.ds(row, BLOCK_TOKENS), columns]
            into = out.at[:, pl.ds(entry * BLOCK_TOKENS, BLOCK_TOKENS)]
            act(pltpu.make_async_copy(source, into, sems.at[h, dest, entry]))

    def all_of(act):
        at = 0
        for h, form in enumerate(forms):
            mine = outs[at : at + count_of(form, rows_of)]
            at += len(mine)
            if form == "shard":

                @pl.loop(seq + 1, n_seq)
                def _(dest):
                    each(h, dest, mine[0].at[dest], act)

            else:
                for ahead, m in entries(rows_of):
                    dest = (seq // near + ahead) * near + jnp.bitwise_xor(seq % near, m)

                    @pl.when((dest > seq) & (dest < n_seq))
                    def _():
                        each(h, dest, entry_of(form, mine, ahead, m), act)

    all_of(lambda copy: copy.start())
    all_of(lambda copy: copy.wait())


def regroup_kernel(shape, place, *refs):
    n_seq, form, into, back, passed = shape
    rows_of = n_seq // NEAR
    n_in, n_out = count_of(form, rows_of), count_of(into, rows_of)
    ins, refs = refs[:n_in], refs[n_in + passed :]
    outs, bufs = refs[:n_out], refs[n_out + passed : -2]
    load_sems, sems = refs[-2:]
    row = place[0] // NEAR
    loads = [pltpu.make_async_copy(ins[i], bufs[i], load_sems.at[i]) for i in range(n_in)]

    def stores(act):
        for ahead, m in entries(rows_of):

            @pl.when((row - ahead >= 0) if back else (row + ahead < rows_of))
            def _():
                ends = entry_of(form, bufs, ahead, m), entry_of(into, outs, ahead, m)
                act(pltpu.make_async_copy(*ends, sems.at[ahead, m]))

    for copy in loads:
        copy.start()
    for copy in loads:
        copy.wait()
    stores(lambda copy: copy.start())
    stores(lambda copy: copy.wait())


def attend_scratch(n_seq, tokens, group_heads, repeat):
    blocks_here = tokens // BLOCK_TOKENS
    rows, columns = repeat * BLOCK_TOKENS, STEP_BLOCKS * BLOCK_TOKENS
    steps = LISTED_ENTRIES // STEP_BLOCKS + 1
    units = group_heads * blocks_here * steps + 5
    return [
        pltpu.VMEM((group_heads, tokens, repeat * HEAD_WIDTH), jnp.bfloat16),
        pltpu.VMEM(
            (group_heads, 2, (n_seq * CAP + blocks_here) * BLOCK_TOKENS, HEAD_WIDTH), jnp.bfloat16
        ),
        pltpu.VMEM((group_heads, tokens + BLOCK_TOKENS, repeat * HEAD_WIDTH), jnp.bfloat16),
        pltpu.VMEM((rows, columns), jnp.float32),
        pltpu.VMEM((rows, columns), jnp.float32),
        pltpu.VMEM((rows, columns), jnp.bfloat16),
        pltpu.VMEM((rows, columns), jnp.bfloat16),
        pltpu.VMEM((rows, HEAD_WIDTH), jnp.float32),
        pltpu.VMEM((rows, HEAD_WIDTH), jnp.float32),
        pltpu.VMEM((rows, HEAD_WIDTH), jnp.float32),
        pltpu.VMEM((rows, HEAD_WIDTH), jnp.float32),
        pltpu.SMEM((units, 5), jnp.int32),
        pltpu.SMEM((units, STEP_BLOCKS), jnp.int32),
        pltpu.SemaphoreType.DMA((group_heads, 3)),
        pltpu.SemaphoreType.DMA((n_seq, group_heads)),
        pltpu.SemaphoreType.DMA((group_heads, blocks_here)),
    ]


def attend_kernel(shape, place, choose, live, queries, keys, values, *refs):
    n_seq, n_head, local_heads, repeat, jobs, given, outs = shape
    group_heads = len(jobs)
    pieces = []
    for whose, plane, _, form in jobs:
        count = count_of(form, n_seq // NEAR)
        pieces.append((form, refs[:count] if form != "shard" else [refs[0].at[plane if whose == "plane" else 0]]))
        refs = refs[count:]
    out = refs[given]
    refs = refs[given + outs :]
    q_buf, kv_buf, o_buf = refs[:3]
    scores, weights = refs[3:5], refs[5:7]
    acc, top, total, shrink, units, taken, sems, piece_sems, out_sems = refs[7:]
    tokens = q_buf.shape[1]
    blocks_here = tokens // BLOCK_TOKENS
    seq, head = place[0], place[1]
    first_block = head * blocks_here
    slots = n_seq * CAP
    q_lanes = repeat * HEAD_WIDTH
    piece_rows = CAP * BLOCK_TOKENS
    own_rows = pl.ds(slots * BLOCK_TOKENS, tokens)
    columns = STEP_BLOCKS * BLOCK_TOKENS
    rows = repeat * BLOCK_TOKENS

    def kv_head(h):
        whose, plane, at, _ = jobs[h]
        return (lax.rem(head + plane, n_head) if whose == "turn" else plane) * local_heads + at

    q_heads = [kv_head(h) for h in range(group_heads)]

    loads = []
    for h in range(group_heads):
        q_cols = pl.ds(pl.multiple_of(q_heads[h] * q_lanes, HEAD_WIDTH), q_lanes)
        kv_cols = pl.ds(pl.multiple_of(q_heads[h] * HEAD_WIDTH, HEAD_WIDTH), HEAD_WIDTH)
        loads += [
            pltpu.make_async_copy(queries.at[:, q_cols], q_buf.at[h], sems.at[h, 0]),
            pltpu.make_async_copy(keys.at[:, kv_cols], kv_buf.at[h, 0, own_rows], sems.at[h, 1]),
            pltpu.make_async_copy(values.at[:, kv_cols], kv_buf.at[h, 1, own_rows], sems.at[h, 2]),
        ]

    def piece_do(h, source, piece, act):
        into = pl.ds(pl.multiple_of(source * piece_rows, piece_rows), piece_rows)
        act(pltpu.make_async_copy(piece, kv_buf.at[h, :, into], piece_sems.at[source, h]))

    def pieces_do(act):
        for h, (form, arrays) in enumerate(pieces):
            if form == "shard":

                @pl.loop(0, seq)
                def _(source):
                    piece_do(h, source, arrays[0].at[source], act)

            else:
                for behind, m in entries(n_seq // NEAR):
                    source = (seq // NEAR - behind) * NEAR + jnp.bitwise_xor(seq % NEAR, m)

                    @pl.when((source >= 0) & (source < seq))
                    def _():
                        piece_do(h, source, entry_of(form, arrays, behind, m), act)

    for copy in loads:
        copy.start()
    pieces_do(lambda copy: copy.start())

    def put(unit, h, block, at, last, out_block):
        units[unit, 0] = h
        units[unit, 1] = block
        units[unit, 2] = at
        units[unit, 3] = last
        units[unit, 4] = out_block
        count = live[first_block + block]
        for i in range(STEP_BLOCKS):
            entry = at * STEP_BLOCKS + i
            slot = choose[first_block + block, jnp.clip(entry - 1, 0, LISTED_ENTRIES - 1)]
            dead = (entry == 0) | (entry > count)
            taken[unit, i] = jnp.where(dead, slots + block, slot) * BLOCK_TOKENS

    for fill in range(2):
        put(fill, 0, 0, 0, 0, blocks_here)

    def put_block(i, at_unit):
        h, block = i // blocks_here, i % blocks_here
        steps = (live[first_block + block] + STEP_BLOCKS) // STEP_BLOCKS

        @pl.loop(0, steps)
        def _(at):
            put(at_unit + at, h, block, at, jnp.where(at == steps - 1, 1, 0), block)

        return at_unit + steps

    last_unit = lax.fori_loop(0, group_heads * blocks_here, put_block, jnp.int32(2))
    for fill in range(3):
        put(last_unit + fill, 0, 0, 0, 0, blocks_here)

    for buf in (*scores, *weights, acc, top, total, shrink):
        buf[...] = jnp.zeros_like(buf)

    for copy in loads:
        copy.wait()
    pieces_do(lambda copy: copy.wait())

    factor = math.log2(math.e) / math.sqrt(HEAD_WIDTH)
    column = lax.broadcasted_iota(jnp.int32, (BLOCK_TOKENS, columns), 1)
    row = lax.broadcasted_iota(jnp.int32, (BLOCK_TOKENS, columns), 0)

    def block_rows(block):
        return pl.ds(pl.multiple_of(block * BLOCK_TOKENS, BLOCK_TOKENS), BLOCK_TOKENS)

    def out_copy(h, block):
        at = block_rows(block)
        q_head = q_heads[0]
        for i in range(1, group_heads):
            q_head = jnp.where(h == i, q_heads[i], q_head)
        q_cols = pl.ds(pl.multiple_of(q_head * q_lanes, HEAD_WIDTH), q_lanes)
        return pltpu.make_async_copy(o_buf.at[h, at], out.at[at, q_cols], out_sems.at[h, block])

    def gathered(unit, which):
        h = units[unit, 0]
        parts = []
        for i in range(STEP_BLOCKS):
            at = pl.ds(pl.multiple_of(taken[unit, i], BLOCK_TOKENS), BLOCK_TOKENS)
            parts.append(kv_buf[h, which, at, :])
        return jnp.concatenate(parts, axis=0)

    def turn(unit, now):
        oldest = unit - 2
        mixed = jnp.dot(weights[now][...], gathered(oldest, 1), preferred_element_type=jnp.float32)
        mixed = acc[...] * shrink[...] + mixed
        acc[...] = mixed
        result = (mixed * (1.0 / total[...])).astype(jnp.bfloat16)
        h, at = units[oldest, 0], block_rows(units[oldest, 4])
        for r in range(repeat):
            o_buf[h, at, r * HEAD_WIDTH : (r + 1) * HEAD_WIDTH] = result[
                r * BLOCK_TOKENS : (r + 1) * BLOCK_TOKENS
            ]

        before = unit - 1
        at_step = units[before, 2]
        count = live[first_block + units[before, 1]]
        limit = (count + 1 - at_step * STEP_BLOCKS) * BLOCK_TOKENS
        reach = jnp.where(at_step == 0, 0, columns)
        allowed = (column < limit) & ((column >= BLOCK_TOKENS) | (column <= row + reach))
        old = jnp.where(at_step == 0, MASKED, top[...])
        kept = jnp.where(
            allowed[None], scores[1 - now][...].reshape(repeat, BLOCK_TOKENS, columns), MASKED
        ).reshape(rows, columns)
        high = jnp.maximum(jnp.max(kept, axis=-1, keepdims=True), old)
        fade = jnp.exp2((old - high) * factor)
        parts = [
            jnp.exp2((kept[:, i : i + HEAD_WIDTH] - high) * factor)
            for i in range(0, columns, HEAD_WIDTH)
        ]
        sums = jnp.sum(functools.reduce(jnp.add, parts), axis=-1, keepdims=True)
        for i, part in enumerate(parts):
            weights[1 - now][:, i * HEAD_WIDTH : (i + 1) * HEAD_WIDTH] = part.astype(jnp.bfloat16)
        top[...] = high
        shrink[...] = fade
        total[...] = total[...] * fade + sums

        h, at = units[unit, 0], block_rows(units[unit, 1])
        q = jnp.concatenate(
            [q_buf[h, at, r * HEAD_WIDTH : (r + 1) * HEAD_WIDTH] for r in range(repeat)], axis=0
        )
        scores[now][...] = lax.dot_general(
            q, gathered(unit, 0), (((1,), (1,)), ((), ())), preferred_element_type=jnp.float32
        )

    def send(unit):
        @pl.when(units[unit, 3] == 1)
        def _():
            out_copy(units[unit, 0], units[unit, 1]).start()

    def two_turns(i, carry):
        unit = 2 * i
        turn(unit, 0)
        turn(unit + 1, 1)
        send(unit - 2)
        send(unit - 1)
        return carry

    lax.fori_loop(1, (last_unit + 3) // 2, two_turns, 0)

    for h in range(group_heads):

        @pl.loop(0, blocks_here)
        def _(block):
            out_copy(h, block).wait()


def body(queries, keys, values, fetch_list, choose, live, *, n_seq, n_head):
    tokens, q_width = queries.shape
    kv_heads = keys.shape[1] // HEAD_WIDTH
    repeat = q_width // HEAD_WIDTH // kv_heads
    local_heads = kv_heads // n_head
    rows_of = n_seq // NEAR
    seq, head = lax.axis_index("seq"), lax.axis_index("head")
    wanted = lax.dynamic_index_in_dim(fetch_list, seq, 1, keepdims=False)
    place = jnp.stack([seq, head]).astype(jnp.int32)

    def piece(*lead):
        return jax.ShapeDtypeStruct(lead + (2, CAP * BLOCK_TOKENS, HEAD_WIDTH), jnp.bfloat16)

    def exchange(first, heads):
        others = []
        for turn in range(1, n_head):
            theirs = lax.rem(head + n_head - turn, n_head) * local_heads + first
            part = jnp.stack(
                [
                    lax.dynamic_slice_in_dim(x, theirs * HEAD_WIDTH, heads * HEAD_WIDTH, axis=1)
                    for x in (keys, values)
                ]
            )
            back = [(h, (h + n_head - turn) % n_head) for h in range(n_head)]
            with jax.named_scope(f"other_plane_{first}"):
                others.append(lax.ppermute(part, "head", back))
        return others

    def pick(first, forms, others):
        shapes = []
        for form in forms:
            lengths = [n_seq] if form == "shard" else lengths_of(form, rows_of)
            shapes += [piece(n) for n in lengths]
        heads = len(forms)
        outs = list(
            pl.pallas_call(
                functools.partial(pick_kernel, (n_head, n_seq, forms, tokens, local_heads, first)),
                out_shape=shapes,
                in_specs=[SMEM, SMEM] + [ANY] * (2 + len(others)),
                out_specs=[ANY] * len(shapes),
                scratch_shapes=[
                    pltpu.VMEM((2, n_head * tokens, heads * HEAD_WIDTH), jnp.bfloat16),
                    pltpu.SemaphoreType.DMA((1 + n_head,)),
                    pltpu.SemaphoreType.DMA((heads, n_seq, CAP)),
                ],
                compiler_params=pltpu.CompilerParams(vmem_limit_bytes=VMEM_BYTES),
                cost_estimate=pl.CostEstimate(
                    flops=PICK_FLOPS * heads, bytes_accessed=2**20, transcendentals=0
                ),
                name="pick",
            )(place, wanted, keys, values, *others)
        )
        return [[outs.pop(0) for _ in range(count_of(form, rows_of))] for form in forms]

    def regroup(form, into, back, parts, *passed):
        n_in, n_out = len(parts), count_of(into, rows_of)
        shapes = [piece(n) for n in lengths_of(into, rows_of)]
        outs = pl.pallas_call(
            functools.partial(regroup_kernel, (n_seq, form, into, back, len(passed))),
            out_shape=shapes + [jax.ShapeDtypeStruct(x.shape, x.dtype) for x in passed],
            in_specs=[SMEM] + [ANY] * (n_in + len(passed)),
            out_specs=[ANY] * (n_out + len(passed)),
            scratch_shapes=[pltpu.VMEM(part.shape, part.dtype) for part in parts]
            + [pltpu.SemaphoreType.DMA((n_in,)), pltpu.SemaphoreType.DMA((rows_of, NEAR))],
            input_output_aliases={1 + n_in + i: n_out + i for i in range(len(passed))},
            compiler_params=pltpu.CompilerParams(vmem_limit_bytes=VMEM_BYTES),
            name="regroup",
        )(place, *parts, *passed)
        return list(outs[:n_out]), *outs[n_out:]

    def relay(after, array):
        return pl.pallas_call(
            lambda *refs: None,
            out_shape=jax.ShapeDtypeStruct(array.shape, array.dtype),
            in_specs=[ANY, ANY],
            out_specs=ANY,
            input_output_aliases={1: 0},
            compiler_params=pltpu.CompilerParams(vmem_limit_bytes=VMEM_BYTES),
            name="relay",
        )(after, array)

    def attend(jobs, *passed):
        operands = [place, choose, live, queries, keys, values]
        shapes = []
        for whose, plane, at, form, arrays in jobs:
            operands += arrays
            shapes.append((whose, plane, at, form))
        n = len(operands)
        outs = [queries if x is None else x for x in passed or [None]]
        given = [i for i, x in enumerate(outs) if passed and passed[i] is not None]
        operands += [passed[i] for i in given]
        return pl.pallas_call(
            functools.partial(
                attend_kernel, (n_seq, n_head, local_heads, repeat, tuple(shapes), len(given), len(outs))
            ),
            out_shape=[jax.ShapeDtypeStruct(x.shape, x.dtype) for x in outs],
            in_specs=[SMEM] * 3 + [ANY] * (len(operands) - 3),
            out_specs=[ANY] * len(outs),
            scratch_shapes=attend_scratch(n_seq, tokens, len(jobs), repeat),
            input_output_aliases={n + i: at for i, at in enumerate(given)},
            compiler_params=pltpu.CompilerParams(vmem_limit_bytes=VMEM_BYTES),
            cost_estimate=pl.CostEstimate(
                flops=ATTEND_FLOPS * len(jobs), bytes_accessed=2**20, transcendentals=0
            ),
            name="attend",
        )(*operands)

    def over_rows(arrays, at):
        got = [arrays[0]] + [None] * (rows_of - 1)
        for ahead in ROW_ORDER:
            if arrays[ahead] is None:
                continue
            step = ahead * NEAR
            pairs = [(s, s + step) for s in range(n_seq - step)]
            with jax.named_scope(f"row_{at}_{ahead}"):
                got[ahead] = lax.ppermute(arrays[ahead], "seq", pairs)
        return got

    def in_row(arrays, at):
        got = [arrays[0]]
        for m in range(1, NEAR):
            with jax.named_scope(f"place_{at}_{m}"):
                got.append(lax.ppermute(arrays[m], "seq", [(s, s ^ m) for s in range(n_seq)]))
        return got

    def swap(arrays, at):
        got = []
        for i, array in enumerate(arrays):
            with jax.named_scope(f"swap_{at}_{i}"):
                got.append(lax.ppermute(array, "head", [(0, 1), (1, 0)]))
        return got

    if n_head != 2 or rows_of != 4 or local_heads != 4:
        passed = []
        for at in range(local_heads):
            ((sends,),) = pick(at, ("shard",), exchange(at, 1))
            got = lax.all_to_all(sends, "seq", split_axis=0, concat_axis=0, tiled=True)
            whole = lax.all_gather(got, "head", axis=0, tiled=False)
            for plane in range(n_head):
                passed = attend([("plane", plane, at, "shard", [whole])], *passed)
        return passed[0]

    def direct(at, sends):
        with jax.named_scope(f"shard_{at}"):
            got = lax.all_to_all(sends, "seq", split_axis=0, concat_axis=0, tiled=True)
        return "shard", [got[None]]

    def own(at, imports):
        return ("turn", 0, at) + imports

    def turned(at, imports):
        form, arrays = imports
        return ("turn", 1, at, form, swap(arrays, at))

    others, rest = exchange(0, 1), exchange(1, 3)
    first = direct(0, pick(0, ("shard",), others)[0][0])
    (sends,), (third,), parts = pick(1, ("shard", "shard", "place"), rest)
    second = direct(1, sends)
    first_turned = swap(first[1], 0)
    out, straight = attend([own(0, first)], None, parts[0])
    parts = [straight] + in_row(parts, 3)[1:]
    grouped, third = regroup("place", "row", False, parts, third)
    third = relay(first_turned[0], third)
    third = direct(2, third)
    job = ("turn", 1, 0, "shard", first_turned)
    out, *grouped[1:-1] = attend([job, own(1, second)], out, *grouped[1:-1])
    ends = [(i, i ^ 1) for i in range(NEAR * n_head)]
    with jax.named_scope("swap_far"):
        twin = lax.ppermute(grouped[-1], ("seq", "head"), ends)
    out, grouped[-1], twin = attend([turned(1, second), own(2, third)], out, grouped[-1], twin)
    fourth = over_rows(grouped, 3)
    twin = over_rows([None] * (rows_of - 1) + [twin], 4)[-1]
    (out,) = attend([turned(2, third), own(3, ("row", fourth))], out)
    (out,) = attend([("turn", 1, 3, "row", swap(fourth[:-1], 3) + [twin])], out)
    return out


def solution(mesh):
    placed = (
        P(("seq", "head"), None),
        P(("seq", "head"), None),
        P(("seq", "head"), None),
        P(),
        P("seq", None),
        P("seq"),
    )
    return jax.shard_map(
        functools.partial(body, n_seq=mesh.shape["seq"], n_head=mesh.shape["head"]),
        mesh=mesh,
        in_specs=placed,
        out_specs=P(("seq", "head"), None),
        check_vma=False,
    )
```
